768 devices in a mesh: row: 2 (over core), col: 12 (over z), layer: 32 (over y, x).
Axes of the slice: x: 4, y: 8, z: 12, core: 2. Of those that a mesh axis runs over, the one named last changes fastest.
Arguments:
- a_blocks: bfloat16 [2, 12, 512, 128, 128], P('row', 'col', 'layer'), may hold values from -0.75 to 0.75
- b_blocks: bfloat16 [2, 12, 512, 128, 128], P('row', 'col', 'layer'), may hold values from -0.75 to 0.75
- a_index: int32 [2, 12, 32, 2, 96], P('row', 'col', 'layer'), may hold values from 0 to 15
- b_index: int32 [2, 12, 32, 2, 96], P('row', 'col', 'layer'), may hold values from 0 to 15
- c_index: int32 [2, 12, 32, 2, 96], P('row', 'col', 'layer'), may hold values from 0 to 31
- counts: int32 [2, 12, 32, 2], P('row', 'col', 'layer'), may hold values from 32 to 96, as said below
Outputs:
- product_blocks: float32 [2, 12, 32, 128, 128], P('row', 'col', 'layer')
The draws below stay inside these ranges and needn't reach their ends.
Inputs may be any that keep to these rules, and one draw needn't show every extreme that they name: `counts`: each entry lies between 32 and 96; 96 is reached on some device at some step.
All inputs are finite; a program needn't handle non-finite values.
Results may differ from the reference program's by a relative error of at most 0.0003.
Values may be sent and summed in bfloat16 or wider, within the bound.
No kernel may reach another device: no remote copies, remote signals or barrier semaphores. Data moves between devices by JAX's collectives and lax.ppermute only.
A program may use at most 64 MiB of HBM per device.

```python
import jax
import jax.numpy as jnp
from jax import lax

BS = 128
SLOTS = 16
CSLOTS = 32
TRIP = 96
STEPS = 2
N_ROW = 2
N_COL = 12
N_LAYER = 32


def draw_counts(key, part):
    key = jax.random.fold_in(key, 7)
    first_key, second_key = jax.random.split(key)
    base = jax.random.randint(first_key, (N_ROW, N_COL, N_LAYER, STEPS), TRIP // 3, TRIP + 1)
    total_cells = N_ROW * N_COL * N_LAYER * STEPS
    spot = jax.random.randint(second_key, (), 0, total_cells)
    flat = base.reshape(-1)
    flat = jnp.where(jnp.arange(total_cells) == spot, TRIP, flat)
    return flat.reshape(base.shape).astype(jnp.int32)


def place_ends(array, stream_key, least, largest):
    dims = array.shape
    index_at = [jax.random.randint(jax.random.fold_in(stream_key, axis), (), 0, dims[axis]) for axis in range(len(dims))]
    array = array.at[tuple(index_at)].set(least)
    longest = dims.index(max(dims))
    index_at[longest] = (index_at[longest] + 1) % dims[longest]
    return array.at[tuple(index_at)].set(largest)


def block_levels(key, shape, cuts, least, largest):
    def one(axis_at, shards_of):
        heights = jax.random.uniform(jax.random.fold_in(jax.random.fold_in(key, 6), axis_at), (shards_of,), jnp.float32, least / len(cuts), largest / len(cuts))
        return jnp.repeat(jnp.exp(heights), shape[axis_at] // shards_of).reshape((-1,) + (1,) * (len(shape) - axis_at - 1))

    loudness = one(*cuts[0])
    for cut in cuts[1:]:
        loudness = loudness * one(*cut)
    return loudness


def normal_values(key, shape, spread, reach, pieces=(), kind=jnp.bfloat16):
    entries = jax.random.normal(key, shape, jnp.float32) * spread
    if len(pieces) > 0:
        entries = block_levels(key, shape, pieces, -0.22, 0.18) * entries
    return jnp.clip(entries, min=-reach, max=reach).astype(kind)


def setup_inputs(seed: int = 0) -> dict:
    key_of = jax.random.split(jax.random.key(seed), 7)
    a_blocks = normal_values(key_of[0], (N_ROW, N_COL, N_LAYER * SLOTS, BS, BS), (BS // 2) ** -0.5, 0.75, ((0, 2), (1, 12), (2, 32)))
    b_blocks = normal_values(key_of[1], (N_ROW, N_COL, N_LAYER * SLOTS, BS, BS), (BS // 2) ** -0.5, 0.75, ((0, 2), (1, 12), (2, 32)))
    a_index = place_ends(jax.random.randint(key_of[2], (N_ROW, N_COL, N_LAYER, STEPS, TRIP), 0, SLOTS), jax.random.fold_in(key_of[2], 1), 0, SLOTS - 1).astype(jnp.int32)
    b_index = place_ends(jax.random.randint(key_of[3], (N_ROW, N_COL, N_LAYER, STEPS, TRIP), 0, SLOTS), jax.random.fold_in(key_of[3], 1), 0, SLOTS - 1).astype(jnp.int32)
    c_index = place_ends(jax.random.randint(key_of[4], (N_ROW, N_COL, N_LAYER, STEPS, TRIP), 0, CSLOTS), jax.random.fold_in(key_of[4], 1), 0, CSLOTS - 1).astype(jnp.int32)
    counts = draw_counts(jax.random.fold_in(key_of[6], 71), 0)
    return dict(a_blocks=a_blocks, b_blocks=b_blocks, a_index=a_index, b_index=b_index, c_index=c_index, counts=counts)


def one_panel(a_panel, b_panel, a_idx, b_idx, c_idx, count):
    left = a_panel[a_idx].astype(jnp.float32)
    right = b_panel[b_idx].astype(jnp.float32)
    terms = jnp.einsum("tij,tjk->tik", left, right)
    live = (jnp.arange(a_idx.shape[0]) < count).astype(jnp.float32)
    terms = terms * live[:, None, None]
    return jax.ops.segment_sum(terms, c_idx, num_segments=CSLOTS)


def reference(a_blocks, b_blocks, a_index, b_index, c_index, counts):
    places = N_ROW * N_COL
    a_first = a_blocks.reshape(places, N_LAYER, SLOTS, BS, BS)
    b_first = b_blocks.reshape(places, N_LAYER, SLOTS, BS, BS)
    a_second = jnp.roll(a_blocks, 1, axis=0).reshape(places, N_LAYER, SLOTS, BS, BS)
    b_second = jnp.roll(b_blocks, 1, axis=1).reshape(places, N_LAYER, SLOTS, BS, BS)
    a_flat = a_index.reshape(places, N_LAYER, STEPS, TRIP)
    b_flat = b_index.reshape(places, N_LAYER, STEPS, TRIP)
    c_flat = c_index.reshape(places, N_LAYER, STEPS, TRIP)
    n_flat = counts.reshape(places, N_LAYER, STEPS)

    def place(which):
        total = jnp.zeros((CSLOTS, BS, BS), jnp.float32)
        for layer_id in range(N_LAYER):
            for step in range(STEPS):
                a_use = a_first[which, layer_id] if step == 0 else a_second[which, layer_id]
                b_use = b_first[which, layer_id] if step == 0 else b_second[which, layer_id]
                total = total + one_panel(a_use, b_use, a_flat[which, layer_id, step], b_flat[which, layer_id, step], c_flat[which, layer_id, step], n_flat[which, layer_id, step])
        return total

    result = lax.map(place, jnp.arange(places, dtype=jnp.int32))
    return result.reshape(N_ROW, N_COL, CSLOTS, BS, BS)
```

```python
import functools

import jax
import jax.numpy as jnp
from jax import lax
from jax.experimental import pallas as pl
from jax.experimental.pallas import tpu as pltpu
from jax.sharding import Mesh
from jax.sharding import PartitionSpec as P

BS = 128
SLOTS = 16
CSLOTS = 32
TRIP = 96
UNROLL = 8
NX = 4
NY = 8
TILE = 16
VMEM_BYTES = 48 * 1024 * 1024

IN_VMEM = pl.BlockSpec(memory_space=pltpu.VMEM)
IN_SMEM = pl.BlockSpec(memory_space=pltpu.SMEM)


def multiply(step, a_idx, b_idx, c_idx, counts, a_ref, b_ref, acc):
    count = counts[step]

    def group(g, carry):
        terms = []
        for u in range(UNROLL):
            t = g * UNROLL + u
            term = jnp.dot(
                a_ref[a_idx[step, t]],
                b_ref[b_idx[step, t]],
                preferred_element_type=jnp.float32,
            )
            terms.append((jnp.where(t < count, c_idx[step, t], CSLOTS), term))
        for target, term in terms:
            acc[target] += term
        return carry

    lax.fori_loop(0, (count + UNROLL - 1) // UNROLL, group, 0)


def power(exponent):
    return jnp.exp2(exponent.astype(jnp.float32))


def encoded(block):
    largest = jnp.max(jnp.abs(block), axis=0, keepdims=True)
    exponent = jnp.floor(jnp.log2(jnp.maximum(largest, 1e-36))).astype(jnp.int32) - 14
    half = exponent >> 1
    scaled = (block * power(-half)) * power(half - exponent)
    rounded = jnp.clip(jnp.round(scaled), -32767.0, 32767.0)
    return rounded.astype(jnp.int32).astype(jnp.int16), exponent


def decoded(integers, exponent):
    half = exponent >> 1
    values = integers.astype(jnp.int32).astype(jnp.float32)
    return (values * power(half)) * power(exponent - half)


def first_kernel(a_idx, b_idx, c_idx, counts, a_ref, b_ref, acc):
    acc[...] = jnp.zeros_like(acc)
    multiply(0, a_idx, b_idx, c_idx, counts, a_ref, b_ref, acc)


def second_kernel(a_idx, b_idx, c_idx, counts, a_ref, b_ref, before, out, acc):
    acc[...] = before[...]
    multiply(1, a_idx, b_idx, c_idx, counts, a_ref, b_ref, acc)
    for x in range(NX):
        rows = []
        for y in range(NY):
            integers, exponent = encoded(acc[y * NX + x])
            out[x, y * BS : (y + 1) * BS] = integers
            rows.append(exponent)
        rows.append(jnp.zeros((TILE - NY, BS), jnp.int32))
        out[x, NY * BS :] = jnp.concatenate(rows, axis=0).astype(jnp.int16)


def middle_kernel(arrived, out):
    exponents = [arrived[x, NY * BS :].astype(jnp.int32) for x in range(NX)]
    for y in range(NY):
        total = None
        for x in range(NX):
            part = decoded(arrived[x, y * BS : (y + 1) * BS], exponents[x][y : y + 1])
            total = part if total is None else total + part
        integers, exponent = encoded(total)
        out[y, :BS] = integers
        out[y, BS:] = jnp.broadcast_to(exponent, (TILE, BS)).astype(jnp.int16)


def last_kernel(arrived, out):
    total = None
    for y in range(NY):
        exponent = arrived[y, BS:].astype(jnp.int32)[0:1]
        part = decoded(arrived[y, :BS], exponent)
        total = part if total is None else total + part
    out[...] = total


def call(kernel, out_shape, in_specs, scratch=(), flops=0, moved=0):
    return pl.pallas_call(
        kernel,
        out_shape=out_shape,
        in_specs=in_specs,
        out_specs=IN_VMEM,
        scratch_shapes=scratch,
        cost_estimate=pl.CostEstimate(flops=flops, bytes_accessed=moved, transcendentals=0),
        compiler_params=pltpu.CompilerParams(vmem_limit_bytes=VMEM_BYTES),
    )


def passed_along(block, axis, distance):
    devices = range(lax.axis_size(axis))
    route = [((i - distance) % len(devices), i) for i in devices]
    return lax.ppermute(block, axis, route)


def body(a_blocks, b_blocks, a_index, b_index, c_index, counts):
    a_own = a_blocks[0, 0]
    b_own = b_blocks[0, 0]
    tables = (a_index[0, 0, 0], b_index[0, 0, 0], c_index[0, 0, 0], counts[0, 0, 0])
    b_next = passed_along(b_own, "col", 1)
    a_next = passed_along(a_own, "row", 1)
    flops = 2 * TRIP * BS**3
    sums = (CSLOTS + 1, BS, BS)
    first = call(
        first_kernel,
        jax.ShapeDtypeStruct(sums, jnp.float32),
        [IN_SMEM] * 4 + [IN_VMEM] * 2,
        flops=16 * flops,
        moved=1 << 22,
    )(*tables, a_own, b_own)
    packed = call(
        second_kernel,
        jax.ShapeDtypeStruct((NX, NY * BS + TILE, BS), jnp.int16),
        [IN_SMEM] * 4 + [IN_VMEM] * 3,
        scratch=[pltpu.VMEM(sums, jnp.float32)],
        flops=16 * flops,
        moved=1 << 22,
    )(*tables, a_next, b_next, first)
    arrived = lax.all_to_all(packed, "x", 0, 0, tiled=True)
    packed = call(
        middle_kernel,
        jax.ShapeDtypeStruct((NY, BS + TILE, BS), jnp.int16),
        [IN_VMEM],
    )(arrived)
    arrived = lax.all_to_all(packed, "y", 0, 0, tiled=True)
    owned = call(
        last_kernel,
        jax.ShapeDtypeStruct((BS, BS), jnp.float32),
        [IN_VMEM],
    )(arrived)
    return owned[None, None, None]


def solution(mesh):
    devices = mesh.devices
    shape = devices.shape[:2] + (NY, NX)
    grid = Mesh(devices.reshape(shape), ("row", "col", "y", "x"))
    layer = ("y", "x")
    panel = P("row", "col", layer, None, None)
    return jax.shard_map(
        body,
        mesh=grid,
        in_specs=(panel, panel, panel, panel, panel, P("row", "col", layer, None)),
        out_specs=panel,
        check_vma=False,
    )
```

```python
import functools

import jax
import jax.numpy as jnp
from jax import lax
from jax.experimental import pallas as pl
from jax.experimental.pallas import tpu as pltpu
from jax.sharding import Mesh
from jax.sharding import PartitionSpec as P

BS = 128
SLOTS = 16
CSLOTS = 32
TRIP = 96
UNROLL = 32
FIRST = ('yl', 'x')
SECOND = ('yh',)
N1 = 8
N2 = CSLOTS // N1
TILE = 16
ROOM = 1.0 - 2.0**-14
VMEM_BYTES = 48 * 1024 * 1024

IN_VMEM = pl.BlockSpec(memory_space=pltpu.VMEM)
IN_SMEM = pl.BlockSpec(memory_space=pltpu.SMEM)


def multiply(step, a_idx, b_idx, c_idx, counts, a_ref, b_ref, acc):
    count = counts[step]

    def group(g, carry):
        terms = []
        for u in range(UNROLL):
            t = g * UNROLL + u
            term = jnp.dot(
                a_ref[a_idx[step, t]],
                b_ref[b_idx[step, t]],
                preferred_element_type=jnp.float32,
            )
            terms.append((jnp.where(t < count, c_idx[step, t], CSLOTS), term))
        for target, term in terms:
            acc[target] += term
        return carry

    lax.fori_loop(0, (count + UNROLL - 1) // UNROLL, group, 0)


def power(exponent):
    return jnp.exp2(exponent.astype(jnp.float32))


def encoded(block):
    largest = jnp.max(jnp.abs(block), axis=0, keepdims=True)
    exponent = jnp.floor(jnp.log2(jnp.maximum(largest, 1e-37))).astype(jnp.int32) - 14
    exponent = jnp.maximum(exponent, -126)
    integers = jnp.round(block * (power(-exponent) * ROOM)).astype(jnp.int32)
    return integers.astype(jnp.int16), exponent


def decoded(integers, exponent):
    return integers.astype(jnp.int32).astype(jnp.float32) * (power(exponent) * (1.0 / ROOM))


def first_kernel(a_idx, b_idx, c_idx, counts, a_ref, b_ref, acc):
    acc[...] = jnp.zeros_like(acc)
    multiply(0, a_idx, b_idx, c_idx, counts, a_ref, b_ref, acc)


def second_kernel(a_idx, b_idx, c_idx, counts, a_ref, b_ref, before, out, acc):
    acc[...] = before[...]
    multiply(1, a_idx, b_idx, c_idx, counts, a_ref, b_ref, acc)
    for i in range(N1):
        rows = []
        for j in range(N2):
            integers, exponent = encoded(acc[j * N1 + i])
            out[i, j * BS : (j + 1) * BS] = integers
            rows.append(exponent)
        if N2 < TILE:
            rows.append(jnp.zeros((TILE - N2, BS), jnp.int32))
        out[i, N2 * BS :] = jnp.concatenate(rows, axis=0).astype(jnp.int16)


def middle_kernel(arrived, out):
    exponents = [arrived[i, N2 * BS :].astype(jnp.int32) for i in range(N1)]
    for j in range(N2):
        total = None
        for i in range(N1):
            part = decoded(arrived[i, j * BS : (j + 1) * BS], exponents[i][j : j + 1])
            total = part if total is None else total + part
        integers, exponent = encoded(total)
        out[j, :BS] = integers
        out[j, BS:] = jnp.broadcast_to(exponent, (TILE, BS)).astype(jnp.int16)


def last_kernel(arrived, out):
    total = None
    for j in range(arrived.shape[0]):
        exponent = arrived[j, BS:].astype(jnp.int32)[0:1]
        part = decoded(arrived[j, :BS], exponent)
        total = part if total is None else total + part
    out[...] = total


def call(kernel, out_shape, in_specs, scratch=(), flops=0, moved=0):
    return pl.pallas_call(
        kernel,
        out_shape=out_shape,
        in_specs=in_specs,
        out_specs=IN_VMEM,
        scratch_shapes=scratch,
        cost_estimate=pl.CostEstimate(flops=flops, bytes_accessed=moved, transcendentals=0),
        compiler_params=pltpu.CompilerParams(vmem_limit_bytes=VMEM_BYTES),
    )


def passed_along(block, axis, distance):
    devices = range(lax.axis_size(axis))
    route = [((i - distance) % len(devices), i) for i in devices]
    return lax.ppermute(block, axis, route)


def body(a_blocks, b_blocks, a_index, b_index, c_index, counts):
    a_own = a_blocks[0, 0]
    b_own = b_blocks[0, 0]
    tables = (a_index[0, 0, 0], b_index[0, 0, 0], c_index[0, 0, 0], counts[0, 0, 0])
    b_next = passed_along(b_own, "col", 1)
    flops = 2 * TRIP * BS**3
    sums = (CSLOTS + 1, BS, BS)
    first = call(
        first_kernel,
        jax.ShapeDtypeStruct(sums, jnp.float32),
        [IN_SMEM] * 4 + [IN_VMEM] * 2,
        flops=16 * flops,
        moved=1 << 22,
    )(*tables, a_own, b_own)
    a_own, first = lax.optimization_barrier((a_own, first))
    a_next = passed_along(a_own, "row", 1)
    packed = call(
        second_kernel,
        jax.ShapeDtypeStruct((N1, N2 * BS + TILE, BS), jnp.int16),
        [IN_SMEM] * 4 + [IN_VMEM] * 3,
        scratch=[pltpu.VMEM(sums, jnp.float32)],
        flops=16 * flops,
        moved=1 << 22,
    )(*tables, a_next, b_next, first)
    arrived = lax.all_to_all(packed, FIRST, 0, 0, tiled=True)
    if N2 > 1:
        packed = call(
            middle_kernel,
            jax.ShapeDtypeStruct((N2, BS + TILE, BS), jnp.int16),
            [IN_VMEM],
        )(arrived)
        arrived = lax.all_to_all(packed, SECOND, 0, 0, tiled=True)
    owned = call(
        last_kernel,
        jax.ShapeDtypeStruct((BS, BS), jnp.float32),
        [IN_VMEM],
    )(arrived)
    return owned[None, None, None]


def solution(mesh):
    devices = mesh.devices
    shape = devices.shape[:2] + (4, 2, 4)
    grid = Mesh(devices.reshape(shape), ("row", "col", "yh", "yl", "x"))
    layer = ("yh", "yl", "x")
    panel = P("row", "col", layer, None, None)
    return jax.shard_map(
        body,
        mesh=grid,
        in_specs=(panel, panel, panel, panel, panel, P("row", "col", layer, None)),
        out_specs=panel,
        check_vma=False,
    )
```

```python
import functools

import jax
import jax.numpy as jnp
from jax import lax
from jax.experimental import pallas as pl
from jax.experimental.pallas import tpu as pltpu
from jax.sharding import Mesh
from jax.sharding import PartitionSpec as P

BS = 128
SLOTS = 16
CSLOTS = 32
TRIP = 96
UNROLL = 32
FIRST = ('yl', 'x')
SECOND = ('yh',)
N1 = 8
N2 = CSLOTS // N1
TILE = 16
ROOM = 1.0 - 2.0**-14
VMEM_BYTES = 32 * 1024 * 1024

IN_VMEM = pl.BlockSpec(memory_space=pltpu.VMEM)
IN_SMEM = pl.BlockSpec(memory_space=pltpu.SMEM)


def multiply(step, a_idx, b_idx, c_idx, counts, a_ref, b_ref, acc):
    count = counts[step]

    def group(g, carry):
        terms = []
        for u in range(UNROLL):
            t = g * UNROLL + u
            term = jnp.dot(
                a_ref[a_idx[step, t]],
                b_ref[b_idx[step, t]],
                preferred_element_type=jnp.float32,
            )
            terms.append((jnp.where(t < count, c_idx[step, t], CSLOTS), term))
        for target, term in terms:
            acc[target] += term
        return carry

    lax.fori_loop(0, (count + UNROLL - 1) // UNROLL, group, 0)


def power(exponent):
    return jnp.exp2(exponent.astype(jnp.float32))


def encoded(block):
    largest = jnp.max(jnp.abs(block), axis=0, keepdims=True)
    exponent = jnp.floor(jnp.log2(jnp.maximum(largest, 1e-37))).astype(jnp.int32) - 14
    exponent = jnp.maximum(exponent, -126)
    integers = jnp.round(block * (power(-exponent) * ROOM)).astype(jnp.int32)
    return integers.astype(jnp.int16), exponent


def decoded(integers, exponent):
    return integers.astype(jnp.int32).astype(jnp.float32) * (power(exponent) * (1.0 / ROOM))


def clear_kernel(a_idx, b_idx, c_idx, counts, acc):
    acc[...] = jnp.zeros_like(acc)


def first_kernel(a_idx, b_idx, c_idx, counts, a_ref, b_ref, before, acc):
    acc[...] = jnp.zeros_like(acc)
    multiply(0, a_idx, b_idx, c_idx, counts, a_ref, b_ref, acc)


def second_kernel(row, a_idx, b_idx, c_idx, counts, a_ref, b_first, b_second, before, out, acc):
    acc[...] = before[...]
    for r, b_ref in enumerate((b_first, b_second)):

        @pl.when(row[0] == r)
        def _(b_ref=b_ref):
            multiply(1, a_idx, b_idx, c_idx, counts, a_ref, b_ref, acc)

    for i in range(N1):
        rows = []
        for j in range(N2):
            integers, exponent = encoded(acc[j * N1 + i])
            out[i, j * BS : (j + 1) * BS] = integers
            rows.append(exponent)
        if N2 < TILE:
            rows.append(jnp.zeros((TILE - N2, BS), jnp.int32))
        out[i, N2 * BS :] = jnp.concatenate(rows, axis=0).astype(jnp.int16)


def middle_kernel(arrived, out):
    exponents = [arrived[i, N2 * BS :].astype(jnp.int32) for i in range(N1)]
    for j in range(N2):
        total = None
        for i in range(N1):
            part = decoded(arrived[i, j * BS : (j + 1) * BS], exponents[i][j : j + 1])
            total = part if total is None else total + part
        integers, exponent = encoded(total)
        out[j, :BS] = integers
        out[j, BS:] = jnp.broadcast_to(exponent, (TILE, BS)).astype(jnp.int16)


def last_kernel(arrived, out):
    total = None
    for j in range(arrived.shape[0]):
        exponent = arrived[j, BS:].astype(jnp.int32)[0:1]
        part = decoded(arrived[j, :BS], exponent)
        total = part if total is None else total + part
    out[...] = total


def call(kernel, out_shape, in_specs, scratch=(), aliases=None, flops=0, moved=0):
    return pl.pallas_call(
        kernel,
        out_shape=out_shape,
        in_specs=in_specs,
        out_specs=jax.tree.map(lambda _: IN_VMEM, out_shape),
        scratch_shapes=scratch,
        input_output_aliases=aliases or {},
        cost_estimate=pl.CostEstimate(flops=flops, bytes_accessed=moved, transcendentals=0),
        compiler_params=pltpu.CompilerParams(vmem_limit_bytes=VMEM_BYTES),
    )


def from_row_above(panel):
    return lax.ppermute(panel, "row", [(0, 1), (1, 0)])


def to_next_column(panel, row):
    columns = lax.axis_size("col")
    first = row * columns
    route = [(first + i, first + (i + 1) % columns) for i in range(columns)]
    return lax.ppermute(panel, ("row", "col"), route)


def body(a_blocks, b_blocks, a_index, b_index, c_index, counts):
    a_own = a_blocks[0, 0]
    b_own = b_blocks[0, 0]
    tables = (a_index[0, 0, 0], b_index[0, 0, 0], c_index[0, 0, 0], counts[0, 0, 0])
    row = lax.axis_index("row").astype(jnp.int32)[None]
    flops = 2 * TRIP * BS**3
    sums = jax.ShapeDtypeStruct((CSLOTS + 1, BS, BS), jnp.float32)
    b_first = to_next_column(b_own, 0)
    mark = call(clear_kernel, jax.ShapeDtypeStruct((8, BS), jnp.float32), [IN_SMEM] * 4)(*tables)
    a_later, b_later, mark = lax.optimization_barrier((a_own, b_own, mark))
    a_next = from_row_above(a_later)
    b_second = to_next_column(b_later, 1)
    acc = call(
        first_kernel,
        sums,
        [IN_SMEM] * 4 + [IN_VMEM] * 3,
        flops=16 * flops,
        moved=1 << 22,
    )(*tables, a_own, b_own, mark)
    packed = call(
        second_kernel,
        jax.ShapeDtypeStruct((N1, N2 * BS + TILE, BS), jnp.int16),
        [IN_SMEM] * 5 + [IN_VMEM] * 4,
        scratch=[pltpu.VMEM(sums.shape, jnp.float32)],
        flops=16 * flops,
        moved=1 << 22,
    )(row, *tables, a_next, b_first, b_second, acc)
    arrived = lax.all_to_all(packed, FIRST, 0, 0, tiled=True)
    if N2 > 1:
        packed = call(
            middle_kernel,
            jax.ShapeDtypeStruct((N2, BS + TILE, BS), jnp.int16),
            [IN_VMEM],
        )(arrived)
        arrived = lax.all_to_all(packed, SECOND, 0, 0, tiled=True)
    owned = call(
        last_kernel,
        jax.ShapeDtypeStruct((BS, BS), jnp.float32),
        [IN_VMEM],
    )(arrived)
    return owned[None, None, None]


def solution(mesh):
    devices = mesh.devices
    shape = devices.shape[:2] + (4, 2, 4)
    grid = Mesh(devices.reshape(shape), ("row", "col", "yh", "yl", "x"))
    layer = ("yh", "yl", "x")
    panel = P("row", "col", layer, None, None)
    return jax.shard_map(
        body,
        mesh=grid,
        in_specs=(panel, panel, panel, panel, panel, P("row", "col", layer, None)),
        out_specs=panel,
        check_vma=False,
    )
```

```python
import functools

import jax
import jax.numpy as jnp
from jax import lax
from jax.experimental import pallas as pl
from jax.experimental.pallas import tpu as pltpu
from jax.sharding import Mesh
from jax.sharding import PartitionSpec as P

BS = 128
SLOTS = 16
CSLOTS = 32
TRIP = 96
UNROLL = 32
FIRST = ('yl', 'x')
SECOND = ('yh',)
N1 = 8
N2 = CSLOTS // N1
TILE = 16
ROOM = 1.0 - 2.0**-14
VMEM_BYTES = 32 * 1024 * 1024

IN_VMEM = pl.BlockSpec(memory_space=pltpu.VMEM)
IN_SMEM = pl.BlockSpec(memory_space=pltpu.SMEM)


def multiply(step, a_idx, b_idx, c_idx, counts, a_ref, b_ref, acc):
    count = counts[step]

    def group(g, carry):
        terms = []
        for u in range(UNROLL):
            t = g * UNROLL + u
            term = jnp.dot(
                a_ref[a_idx[step, t]],
                b_ref[b_idx[step, t]],
                preferred_element_type=jnp.float32,
            )
            terms.append((jnp.where(t < count, c_idx[step, t], CSLOTS), term))
        for target, term in terms:
            acc[target] += term
        return carry

    lax.fori_loop(0, (count + UNROLL - 1) // UNROLL, group, 0)


def power(exponent):
    return jnp.exp2(exponent.astype(jnp.float32))


def encoded(block):
    largest = jnp.max(jnp.abs(block), axis=0, keepdims=True)
    exponent = jnp.floor(jnp.log2(jnp.maximum(largest, 1e-37))).astype(jnp.int32) - 14
    exponent = jnp.maximum(exponent, -126)
    integers = jnp.round(block * (power(-exponent) * ROOM)).astype(jnp.int32)
    return integers.astype(jnp.int16), exponent


def decoded(integers, exponent):
    return integers.astype(jnp.int32).astype(jnp.float32) * (power(exponent) * (1.0 / ROOM))


def clear_kernel(a_idx, b_idx, c_idx, counts, acc):
    acc[...] = jnp.zeros_like(acc)


def first_kernel(a_idx, b_idx, c_idx, counts, a_ref, b_ref, before, acc):
    acc[...] = jnp.zeros_like(acc)
    multiply(0, a_idx, b_idx, c_idx, counts, a_ref, b_ref, acc)


def second_kernel(row, a_idx, b_idx, c_idx, counts, b_first, b_second, a_ref, before, out, acc):
    acc[...] = before[...]
    for r, b_ref in enumerate((b_second, b_first)):

        @pl.when(row[0] == r)
        def _(b_ref=b_ref):
            multiply(1, a_idx, b_idx, c_idx, counts, a_ref, b_ref, acc)

    for i in range(N1):
        rows = []
        for j in range(N2):
            integers, exponent = encoded(acc[j * N1 + i])
            out[i, j * BS : (j + 1) * BS] = integers
            rows.append(exponent)
        if N2 < TILE:
            rows.append(jnp.zeros((TILE - N2, BS), jnp.int32))
        out[i, N2 * BS :] = jnp.concatenate(rows, axis=0).astype(jnp.int16)


def middle_kernel(arrived, out):
    exponents = [arrived[i, N2 * BS :].astype(jnp.int32) for i in range(N1)]
    for j in range(N2):
        total = None
        for i in range(N1):
            part = decoded(arrived[i, j * BS : (j + 1) * BS], exponents[i][j : j + 1])
            total = part if total is None else total + part
        integers, exponent = encoded(total)
        out[j, :BS] = integers
        out[j, BS:] = jnp.broadcast_to(exponent, (TILE, BS)).astype(jnp.int16)


def last_kernel(arrived, out):
    total = None
    for j in range(arrived.shape[0]):
        exponent = arrived[j, BS:].astype(jnp.int32)[0:1]
        part = decoded(arrived[j, :BS], exponent)
        total = part if total is None else total + part
    out[...] = total


def call(kernel, out_shape, in_specs, scratch=(), aliases=None, flops=0, moved=0):
    return pl.pallas_call(
        kernel,
        out_shape=out_shape,
        in_specs=in_specs,
        out_specs=jax.tree.map(lambda _: IN_VMEM, out_shape),
        scratch_shapes=scratch,
        input_output_aliases=aliases or {},
        cost_estimate=pl.CostEstimate(flops=flops, bytes_accessed=moved, transcendentals=0),
        compiler_params=pltpu.CompilerParams(vmem_limit_bytes=VMEM_BYTES),
    )


def from_row_above(panel):
    return lax.ppermute(panel, "row", [(0, 1), (1, 0)])


def to_next_column(panel, row):
    columns = lax.axis_size("col")
    first = row * columns
    route = [(first + i, first + (i + 1) % columns) for i in range(columns)]
    return lax.ppermute(panel, ("row", "col"), route)


def body(a_blocks, b_blocks, a_index, b_index, c_index, counts):
    a_own = a_blocks[0, 0]
    b_own = b_blocks[0, 0]
    tables = (a_index[0, 0, 0], b_index[0, 0, 0], c_index[0, 0, 0], counts[0, 0, 0])
    row = lax.axis_index("row").astype(jnp.int32)[None]
    flops = 2 * TRIP * BS**3
    sums = jax.ShapeDtypeStruct((CSLOTS + 1, BS, BS), jnp.float32)
    b_first = to_next_column(b_own, 1)
    mark = call(clear_kernel, jax.ShapeDtypeStruct((8, BS), jnp.float32), [IN_SMEM] * 4)(*tables)
    a_later, b_later, mark = lax.optimization_barrier((a_own, b_own, mark))
    a_next = from_row_above(a_later)
    b_second = to_next_column(b_later, 0)
    acc = call(
        first_kernel,
        sums,
        [IN_SMEM] * 4 + [IN_VMEM] * 3,
        flops=16 * flops,
        moved=1 << 22,
    )(*tables, a_own, b_own, mark)
    packed = call(
        second_kernel,
        jax.ShapeDtypeStruct((N1, N2 * BS + TILE, BS), jnp.int16),
        [IN_SMEM] * 5 + [IN_VMEM] * 4,
        scratch=[pltpu.VMEM(sums.shape, jnp.float32)],
        flops=16 * flops,
        moved=1 << 22,
    )(row, *tables, b_first, b_second, a_next, acc)
    arrived = lax.all_to_all(packed, FIRST, 0, 0, tiled=True)
    if N2 > 1:
        packed = call(
            middle_kernel,
            jax.ShapeDtypeStruct((N2, BS + TILE, BS), jnp.int16),
            [IN_VMEM],
        )(arrived)
        arrived = lax.all_to_all(packed, SECOND, 0, 0, tiled=True)
    owned = call(
        last_kernel,
        jax.ShapeDtypeStruct((BS, BS), jnp.float32),
        [IN_VMEM],
    )(arrived)
    return owned[None, None, None]


def solution(mesh):
    devices = mesh.devices
    shape = devices.shape[:2] + (4, 2, 4)
    grid = Mesh(devices.reshape(shape), ("row", "col", "yh", "yl", "x"))
    layer = ("yh", "yl", "x")
    panel = P("row", "col", layer, None, None)
    return jax.shard_map(
        body,
        mesh=grid,
        in_specs=(panel, panel, panel, panel, panel, P("row", "col", layer, None)),
        out_specs=panel,
        check_vma=False,
    )
```

```python
import functools

import jax
import jax.numpy as jnp
from jax import lax
from jax.experimental import pallas as pl
from jax.experimental.pallas import tpu as pltpu
from jax.sharding import Mesh
from jax.sharding import PartitionSpec as P

BS = 128
SLOTS = 16
CSLOTS = 32
TRIP = 96
UNROLL = 32
FIRST = ('yl', 'x')
SECOND = ('yh',)
N1 = 8
N2 = CSLOTS // N1
TILE = 16
ROOM = 1.0 - 2.0**-8
VMEM_BYTES = 32 * 1024 * 1024

IN_VMEM = pl.BlockSpec(memory_space=pltpu.VMEM)
IN_SMEM = pl.BlockSpec(memory_space=pltpu.SMEM)


def multiply(step, a_idx, b_idx, c_idx, counts, a_ref, b_ref, acc):
    count = counts[step]

    def group(g, carry):
        terms = []
        for u in range(UNROLL):
            t = g * UNROLL + u
            term = jnp.dot(
                a_ref[a_idx[step, t]],
                b_ref[b_idx[step, t]],
                preferred_element_type=jnp.float32,
            )
            terms.append((jnp.where(t < count, c_idx[step, t], CSLOTS), term))
        for target, term in terms:
            acc[target] += term
        return carry

    lax.fori_loop(0, (count + UNROLL - 1) // UNROLL, group, 0)


def power(exponent):
    return jnp.exp2(exponent.astype(jnp.float32))


def encoded(block):
    largest = jnp.max(jnp.abs(block), axis=0, keepdims=True)
    exponent = jnp.floor(jnp.log2(jnp.maximum(largest, 1e-37))).astype(jnp.int32) - 14
    exponent = jnp.maximum(exponent, -126)
    integers = jnp.round(block * (power(-exponent) * ROOM)).astype(jnp.int32)
    return integers.astype(jnp.int16), exponent


def decoded(integers, exponent):
    return integers.astype(jnp.int32).astype(jnp.float32) * (power(exponent) * (1.0 / ROOM))


def clear_kernel(a_idx, b_idx, c_idx, counts, a_ref, b_ref, acc):
    acc[...] = jnp.zeros_like(acc)


def first_kernel(a_idx, b_idx, c_idx, counts, a_ref, b_ref, before, acc):
    acc[...] = jnp.zeros_like(acc)
    multiply(0, a_idx, b_idx, c_idx, counts, a_ref, b_ref, acc)


def second_kernel(row, a_idx, b_idx, c_idx, counts, b_first, b_second, a_ref, before, out, acc):
    acc[...] = before[...]
    for r, b_ref in enumerate((b_second, b_first)):

        @pl.when(row[0] == r)
        def _(b_ref=b_ref):
            multiply(1, a_idx, b_idx, c_idx, counts, a_ref, b_ref, acc)

    for i in range(N1):
        rows = []
        for j in range(N2):
            integers, exponent = encoded(acc[j * N1 + i])
            out[i, j * BS : (j + 1) * BS] = integers
            rows.append(exponent)
        if N2 < TILE:
            rows.append(jnp.zeros((TILE - N2, BS), jnp.int32))
        out[i, N2 * BS :] = jnp.concatenate(rows, axis=0).astype(jnp.int16)


def middle_kernel(arrived, out):
    exponents = [arrived[i, N2 * BS :].astype(jnp.int32) for i in range(N1)]
    for j in range(N2):
        total = None
        for i in range(N1):
            part = decoded(arrived[i, j * BS : (j + 1) * BS], exponents[i][j : j + 1])
            total = part if total is None else total + part
        integers, exponent = encoded(total)
        out[j, :BS] = integers
        out[j, BS:] = jnp.broadcast_to(exponent, (TILE, BS)).astype(jnp.int16)


def last_kernel(arrived, out):
    total = None
    for j in range(arrived.shape[0]):
        exponent = arrived[j, BS:].astype(jnp.int32)[0:1]
        part = decoded(arrived[j, :BS], exponent)
        total = part if total is None else total + part
    out[...] = total


def call(kernel, out_shape, in_specs, scratch=(), aliases=None, flops=0, moved=0):
    return pl.pallas_call(
        kernel,
        out_shape=out_shape,
        in_specs=in_specs,
        out_specs=jax.tree.map(lambda _: IN_VMEM, out_shape),
        scratch_shapes=scratch,
        input_output_aliases=aliases or {},
        cost_estimate=pl.CostEstimate(flops=flops, bytes_accessed=moved, transcendentals=0),
        compiler_params=pltpu.CompilerParams(vmem_limit_bytes=VMEM_BYTES),
    )


def from_row_above(panel):
    return lax.ppermute(panel, "row", [(0, 1), (1, 0)])


def to_next_column(panel, row):
    columns = lax.axis_size("col")
    first = row * columns
    route = [(first + i, first + (i + 1) % columns) for i in range(columns)]
    return lax.ppermute(panel, ("row", "col"), route)


def body(a_blocks, b_blocks, a_index, b_index, c_index, counts):
    a_own = a_blocks[0, 0]
    b_own = b_blocks[0, 0]
    tables = (a_index[0, 0, 0], b_index[0, 0, 0], c_index[0, 0, 0], counts[0, 0, 0])
    row = lax.axis_index("row").astype(jnp.int32)[None]
    flops = 2 * TRIP * BS**3
    sums = jax.ShapeDtypeStruct((CSLOTS + 1, BS, BS), jnp.float32)
    b_first = to_next_column(b_own, 1)
    mark = call(clear_kernel, jax.ShapeDtypeStruct((8, BS), jnp.float32), [IN_SMEM] * 4 + [IN_VMEM] * 2)(*tables, a_own, b_own)
    a_later, b_later, mark = lax.optimization_barrier((a_own, b_own, mark))
    a_next = from_row_above(a_later)
    b_second = to_next_column(b_later, 0)
    acc = call(
        first_kernel,
        sums,
        [IN_SMEM] * 4 + [IN_VMEM] * 3,
        flops=16 * flops,
        moved=1 << 22,
    )(*tables, a_own, b_own, mark)
    packed = call(
        second_kernel,
        jax.ShapeDtypeStruct((N1, N2 * BS + TILE, BS), jnp.int16),
        [IN_SMEM] * 5 + [IN_VMEM] * 4,
        scratch=[pltpu.VMEM(sums.shape, jnp.float32)],
        flops=16 * flops,
        moved=1 << 22,
    )(row, *tables, b_first, b_second, a_next, acc)
    arrived = lax.all_to_all(packed, FIRST, 0, 0, tiled=True)
    if N2 > 1:
        packed = call(
            middle_kernel,
            jax.ShapeDtypeStruct((N2, BS + TILE, BS), jnp.int16),
            [IN_VMEM],
        )(arrived)
        arrived = lax.all_to_all(packed, SECOND, 0, 0, tiled=True)
    owned = call(
        last_kernel,
        jax.ShapeDtypeStruct((BS, BS), jnp.float32),
        [IN_VMEM],
    )(arrived)
    return owned[None, None, None]


def solution(mesh):
    devices = mesh.devices
    shape = devices.shape[:2] + (4, 2, 4)
    grid = Mesh(devices.reshape(shape), ("row", "col", "yh", "yl", "x"))
    layer = ("yh", "yl", "x")
    panel = P("row", "col", layer, None, None)
    return jax.shard_map(
        body,
        mesh=grid,
        in_specs=(panel, panel, panel, panel, panel, P("row", "col", layer, None)),
        out_specs=panel,
        check_vma=False,
    )
```

```python
import functools

import jax
import jax.numpy as jnp
from jax import lax
from jax.experimental import pallas as pl
from jax.experimental.pallas import tpu as pltpu
from jax.sharding import Mesh
from jax.sharding import PartitionSpec as P

BS = 128
SLOTS = 16
CSLOTS = 32
TRIP = 96
UNROLL = 32
FIRST = ('yl', 'x')
SECOND = ('yh',)
N1 = 8
N2 = CSLOTS // N1
TILE = 16
ROOM = 1.0 - 2.0**-8
VMEM_BYTES = 32 * 1024 * 1024

IN_VMEM = pl.BlockSpec(memory_space=pltpu.VMEM)
IN_SMEM = pl.BlockSpec(memory_space=pltpu.SMEM)


def multiply(step, a_idx, b_idx, c_idx, counts, a_ref, b_ref, acc):
    count = counts[step]

    def group(g, carry):
        terms = []
        for u in range(UNROLL):
            t = g * UNROLL + u
            term = jnp.dot(
                a_ref[a_idx[step, t]],
                b_ref[b_idx[step, t]],
                preferred_element_type=jnp.float32,
            )
            terms.append((jnp.where(t < count, c_idx[step, t], CSLOTS), term))
        for target, term in terms:
            acc[target] += term
        return carry

    lax.fori_loop(0, (count + UNROLL - 1) // UNROLL, group, 0)


def power(exponent):
    return jnp.exp2(exponent.astype(jnp.float32))


def encoded(block):
    largest = jnp.max(jnp.abs(block), axis=0, keepdims=True)
    exponent = jnp.floor(jnp.log2(jnp.maximum(largest, 1e-37))).astype(jnp.int32) - 14
    exponent = jnp.maximum(exponent, -126)
    integers = jnp.round(block * (power(-exponent) * ROOM)).astype(jnp.int32)
    return integers.astype(jnp.int16), exponent


def decoded(integers, exponent):
    return integers.astype(jnp.int32).astype(jnp.float32) * (power(exponent) * (1.0 / ROOM))


def clear_kernel(a_idx, b_idx, c_idx, counts, a_ref, b_ref, acc):
    acc[...] = jnp.zeros_like(acc)


def first_kernel(a_idx, b_idx, c_idx, counts, a_ref, b_ref, before, acc):
    acc[...] = jnp.zeros_like(acc)
    multiply(0, a_idx, b_idx, c_idx, counts, a_ref, b_ref, acc)


def second_kernel(row, a_idx, b_idx, c_idx, counts, b_first, b_second, a_ref, before, out, acc):
    for r, b_ref in enumerate((b_second, b_first)):

        @pl.when(row[0] == r)
        def _(b_ref=b_ref):
            multiply(1, a_idx, b_idx, c_idx, counts, a_ref, b_ref, acc)

    for i in range(N1):
        rows = []
        for j in range(N2):
            integers, exponent = encoded(acc[j * N1 + i])
            out[i, j * BS : (j + 1) * BS] = integers
            rows.append(exponent)
        if N2 < TILE:
            rows.append(jnp.zeros((TILE - N2, BS), jnp.int32))
        out[i, N2 * BS :] = jnp.concatenate(rows, axis=0).astype(jnp.int16)


def middle_kernel(arrived, out):
    exponents = [arrived[i, N2 * BS :].astype(jnp.int32) for i in range(N1)]
    for j in range(N2):
        total = None
        for i in range(N1):
            part = decoded(arrived[i, j * BS : (j + 1) * BS], exponents[i][j : j + 1])
            total = part if total is None else total + part
        integers, exponent = encoded(total)
        out[j, :BS] = integers
        out[j, BS:] = jnp.broadcast_to(exponent, (TILE, BS)).astype(jnp.int16)


def last_kernel(arrived, out):
    total = None
    for j in range(arrived.shape[0]):
        exponent = arrived[j, BS:].astype(jnp.int32)[0:1]
        part = decoded(arrived[j, :BS], exponent)
        total = part if total is None else total + part
    out[...] = total


def call(kernel, out_shape, in_specs, scratch=(), aliases=None, flops=0, moved=0):
    return pl.pallas_call(
        kernel,
        out_shape=out_shape,
        in_specs=in_specs,
        out_specs=jax.tree.map(lambda _: IN_VMEM, out_shape),
        scratch_shapes=scratch,
        input_output_aliases=aliases or {},
        cost_estimate=pl.CostEstimate(flops=flops, bytes_accessed=moved, transcendentals=0),
        compiler_params=pltpu.CompilerParams(vmem_limit_bytes=VMEM_BYTES),
    )


def from_row_above(panel):
    return lax.ppermute(panel, "row", [(0, 1), (1, 0)])


def to_next_column(panel, row):
    columns = lax.axis_size("col")
    first = row * columns
    route = [(first + i, first + (i + 1) % columns) for i in range(columns)]
    return lax.ppermute(panel, ("row", "col"), route)


def body(a_blocks, b_blocks, a_index, b_index, c_index, counts):
    a_own = a_blocks[0, 0]
    b_own = b_blocks[0, 0]
    tables = (a_index[0, 0, 0], b_index[0, 0, 0], c_index[0, 0, 0], counts[0, 0, 0])
    row = lax.axis_index("row").astype(jnp.int32)[None]
    flops = 2 * TRIP * BS**3
    sums = jax.ShapeDtypeStruct((CSLOTS + 1, BS, BS), jnp.float32)
    b_first = to_next_column(b_own, 1)
    mark = call(clear_kernel, jax.ShapeDtypeStruct((8, BS), jnp.float32), [IN_SMEM] * 4 + [IN_VMEM] * 2)(*tables, a_own, b_own)
    a_later, b_later, mark = lax.optimization_barrier((a_own, b_own, mark))
    a_next = from_row_above(a_later)
    b_second = to_next_column(b_later, 0)
    acc = call(
        first_kernel,
        sums,
        [IN_SMEM] * 4 + [IN_VMEM] * 3,
        flops=16 * flops,
        moved=1 << 22,
    )(*tables, a_own, b_own, mark)
    packed, _ = call(
        second_kernel,
        (jax.ShapeDtypeStruct((N1, N2 * BS + TILE, BS), jnp.int16), sums),
        [IN_SMEM] * 5 + [IN_VMEM] * 4,
        aliases={8: 1},
        flops=16 * flops,
        moved=1 << 22,
    )(row, *tables, b_first, b_second, a_next, acc)
    arrived = lax.all_to_all(packed, FIRST, 0, 0, tiled=True)
    if N2 > 1:
        packed = call(
            middle_kernel,
            jax.ShapeDtypeStruct((N2, BS + TILE, BS), jnp.int16),
            [IN_VMEM],
        )(arrived)
        arrived = lax.all_to_all(packed, SECOND, 0, 0, tiled=True)
    owned = call(
        last_kernel,
        jax.ShapeDtypeStruct((BS, BS), jnp.float32),
        [IN_VMEM],
    )(arrived)
    return owned[None, None, None]


def solution(mesh):
    devices = mesh.devices
    shape = devices.shape[:2] + (4, 2, 4)
    grid = Mesh(devices.reshape(shape), ("row", "col", "yh", "yl", "x"))
    layer = ("yh", "yl", "x")
    panel = P("row", "col", layer, None, None)
    return jax.shard_map(
        body,
        mesh=grid,
        in_specs=(panel, panel, panel, panel, panel, P("row", "col", layer, None)),
        out_specs=panel,
        check_vma=False,
    )
```
